32 devices in a mesh: parts: 2 (over y), wide: 8 (over z, x), narrow: 2 (over core).
Axes of the slice: x: 2, y: 2, z: 4, core: 2. Of those that a mesh axis runs over, the one named last changes fastest.
Arguments:
- state: float32 [128, 64, 256], P(('parts', 'wide'), 'narrow'), parts along dimension 0, may hold values from -6 to 6
- permeability: float32 [128, 64, 256], P(('parts', 'wide'), 'narrow'), parts along dimension 0, may hold values from 0.3 to 3
- direction: float32 [128, 64, 256], P(('parts', 'wide'), 'narrow'), parts along dimension 0, may hold values from -6 to 6
- obs_weight: float32 [128, 64, 256], P(('parts', 'wide'), 'narrow'), parts along dimension 0, may hold values from 0.5 to 5
- coarse_inverse: float32 [32, 16], P('parts'), parts along dimension 0, as said below
Outputs:
- hessian_action: float32 [128, 64, 256], P(('parts', 'wide'), 'narrow'), parts along dimension 0
- increment: float32 [128, 64, 256], P(('parts', 'wide'), 'narrow'), parts along dimension 0
The draws below stay inside these ranges and needn't reach their ends.
There are 2 independent parts, one for each index of `parts`. The reference program is written for one: setup_inputs(seed, part) draws one part's arguments, and reference() takes and returns one part's arrays. A program takes and returns all parts, laid end to end along the dimension named above; each array names one. Nothing has to cross between parts.
Inputs may be any that keep to these rules, and one draw needn't show every extreme that they name: `coarse_inverse`: a given dense matrix over bricks, not derived from the permeability.
All inputs are finite; a program needn't handle non-finite values.
Results may differ from the reference program's by a relative error of at most 0.0003.
Values sent between devices are 32-bit elements; how exact they have to be, the bound alone decides.
A program may use at most 128 MiB of HBM per device.

```python
import math
import jax
import jax.numpy as jnp
from jax import lax

CX = 8
CY = 32
CZ = 256
NX = 64
NY = 64
NZ = 256
BRICKS = 16
N_WIDE = 8
N_NARROW = 2


def draw_coarse_inverse(key, part):
    key = jax.random.fold_in(key, 11)
    noise = jax.random.normal(key, (BRICKS, BRICKS), jnp.float32) * 0.7
    identity = jnp.eye(BRICKS, dtype=jnp.float32)
    factor = 64.0 / (CX * CY * CZ)
    return factor * (2.0 * identity + noise * BRICKS ** (-0.5))


def level_of(rng, shape, pieces, least, top_value):
    gain, own = 1.0, jax.random.fold_in(rng, 6)
    for position, parts in pieces:
        steps = jnp.exp(jax.random.uniform(jax.random.fold_in(own, position), (parts,), jnp.float32, least / len(pieces), top_value / len(pieces)))
        gain = gain * jnp.repeat(steps, shape[position] // parts).reshape([-1 if axis == position else 1 for axis in range(len(shape))])
    return gain


def gaussian(own_key, extent, spread, limit, shards=(), held_as=jnp.bfloat16):
    result = spread * jax.random.normal(own_key, extent, jnp.float32)
    if shards:
        result = result * level_of(own_key, extent, shards, -0.22, 0.18)
    return jnp.clip(result, -limit, limit).astype(held_as)


def setup_inputs(seed: int = 0, part: int = 0) -> dict:
    streams_of = jax.random.split(jax.random.key(seed), 6)
    part_splits = jax.random.split(jax.random.fold_in(streams_of[5], part), 6)
    return {
        "state": gaussian(part_splits[0], (NX, NY, NZ), 1.0, 6.0, ((0, 8), (1, 2)), jnp.float32),
        "permeability": jnp.clip(jnp.exp(math.log(3.0) - 2.3025851 * jax.random.uniform(part_splits[1], (NX, NY, NZ), jnp.float32) ** level_of(part_splits[1], (NX, NY, NZ), ((0, 8), (1, 2)), -0.2, 0.2)), 0.3, 3.0),
        "direction": gaussian(part_splits[2], (NX, NY, NZ), 1.0, 6.0, ((0, 8), (1, 2)), jnp.float32),
        "obs_weight": jnp.clip(jnp.exp(math.log(5.0) - 2.3025851 * jax.random.uniform(part_splits[3], (NX, NY, NZ), jnp.float32) ** level_of(part_splits[3], (NX, NY, NZ), ((0, 8), (1, 2)), -0.2, 0.2)), 0.5, 5.0),
        "coarse_inverse": draw_coarse_inverse(jax.random.fold_in(jax.random.fold_in(streams_of[5], part), 71), part),
    }


cheb_mid = 1.125
cheb_half = 0.875
first_rho = cheb_half / cheb_mid
second_rho = 1.0 / (2.0 * cheb_mid / cheb_half - first_rho)
step_gain = 2.0 * second_rho / cheb_half
carry_gain = second_rho * first_rho


def pad_depth(values):
    return jnp.pad(values, ((0, 0), (0, 0), (1, 1)))


def pad_plane(values):
    return jnp.pad(values, ((1, 1), (1, 1), (0, 0)))


def neighbour_list(padded):
    middle = padded[1:-1, 1:-1]
    deeper = pad_depth(middle)
    return middle, [padded[2:, 1:-1], padded[:-2, 1:-1], padded[1:-1, 2:], padded[1:-1, :-2], deeper[:, :, 2:], deeper[:, :, :-2]]


def apply_pad(padded, coeff_pad, factor):
    middle, beside_all = neighbour_list(padded)
    own_coeff, coeff_around = neighbour_list(coeff_pad)
    summed = jnp.zeros_like(middle)
    for beside, beside_coeff in zip(beside_all, coeff_around):
        summed = summed + 0.5 * (own_coeff + beside_coeff) * (middle - beside)
    return factor * summed


def diagonal_pad(coeff_pad, factor):
    own_coeff, coeff_around = neighbour_list(coeff_pad)
    summed = jnp.zeros_like(own_coeff)
    for beside_coeff in coeff_around:
        summed = summed + 0.5 * (own_coeff + beside_coeff)
    return factor * summed


def hessian_pad(state_pad, adjoint_pad, permeability):
    state_mid, state_around = neighbour_list(state_pad)
    adjoint_mid, adjoint_around = neighbour_list(adjoint_pad)
    summed = jnp.zeros_like(state_mid)
    for state_side, adjoint_side in zip(state_around, adjoint_around):
        summed = summed + (state_mid - state_side) * (adjoint_mid - adjoint_side)
    return 0.5 * permeability * summed


def coarsen(values):
    first, second, third = values.shape
    return values.reshape(first // 2, 2, second // 2, 2, third // 2, 2).mean(axis=(1, 3, 5))


def refine(values):
    return jnp.repeat(jnp.repeat(jnp.repeat(values, 2, 0), 2, 1), 2, 2)


def smooth(start, target, operate, inverse_diag):
    resid = target - operate(start)
    update = inverse_diag * resid / cheb_mid
    iterate = start + update
    resid = target - operate(iterate)
    update = carry_gain * update + step_gain * inverse_diag * resid
    return iterate + update


def reference(state, permeability, direction, obs_weight, coarse_inverse):
    k_pad = pad_plane(permeability)
    coarse_k_pad = pad_plane(coarsen(permeability))
    inv_fine = 1.0 / diagonal_pad(k_pad, 1.0)
    inv_coarse = 1.0 / diagonal_pad(coarse_k_pad, 0.25)

    def fine_apply(values):
        return apply_pad(pad_plane(values), k_pad, 1.0)

    def coarse_apply(values):
        return apply_pad(pad_plane(values), coarse_k_pad, 0.25)

    def vcycle(target):
        iterate = smooth(jnp.zeros_like(target), target, fine_apply, inv_fine)
        coarse_target = coarsen(target - fine_apply(iterate))
        coarse_iter = smooth(jnp.zeros_like(coarse_target), coarse_target, coarse_apply, inv_coarse)
        leftover = coarse_target - coarse_apply(coarse_iter)
        shape5 = (N_WIDE, CX // 2, N_NARROW, CY // 2, NZ // 2)
        totals = leftover.reshape(shape5).sum(axis=(1, 3, 4)).reshape(-1)
        correction = jnp.dot(coarse_inverse, totals, precision=lax.Precision.HIGHEST)
        coarse_iter = (coarse_iter.reshape(shape5) + correction.reshape(N_WIDE, 1, N_NARROW, 1, 1)).reshape(coarse_target.shape)
        coarse_iter = smooth(coarse_iter, coarse_target, coarse_apply, inv_coarse)
        iterate = iterate + refine(coarse_iter)
        return smooth(iterate, target, fine_apply, inv_fine)

    source = -apply_pad(pad_plane(state), pad_plane(direction * permeability), 1.0)
    increment = vcycle(source)
    adjoint = vcycle(-(obs_weight * increment))
    hessian = hessian_pad(pad_plane(state), pad_plane(adjoint), permeability)
    return hessian, increment
```

```python
import functools

import jax
import jax.numpy as jnp
from jax import lax
from jax.experimental import pallas as pl
from jax.experimental.pallas import tpu as pltpu
from jax.sharding import PartitionSpec as P

MESH = pl.DeviceIdType.MESH
f32 = jnp.float32
bf16 = jnp.bfloat16

cheb_mid = 1.125
cheb_half = 0.875
first_rho = cheb_half / cheb_mid
second_rho = 1.0 / (2.0 * cheb_mid / cheb_half - first_rho)
step_gain = 2.0 * second_rho / cheb_half
carry_gain = second_rho * first_rho
inv_mid = 1.0 / cheb_mid


def split3(a):
    hi = a.astype(bf16)
    rest = a - hi.astype(f32)
    mid = rest.astype(bf16)
    low = (rest - mid.astype(f32)).astype(bf16)
    return hi, mid, low


def permuted(a, perm):
    parts = [jnp.dot(s, perm, preferred_element_type=f32) for s in split3(a)]
    return parts[0] + (parts[1] + parts[2])


def kernel(n, nb, state_in, k_in, dir_in, w_in, inv_in, hess_out, inc_out, stage, t_s, t_k, t_c, t_w, s_r, k_r, c_r, w_r,
           czi, czo, cyi, cyo, cx, dia, inv, b_r, x1_r, x2_r, xa, xb, upd, kc, ccx, ccy, ccz, diac, invc, g_r, y1, y2_r,
           ya, yb, updc, tot, corr, adj, o_inc, o_hess, r_inc, r_hess, send_sem, recv_sem):
    wide = lax.axis_index("wide")
    core = lax.axis_index("narrow")
    n_wide = n // 2
    p = 2 * wide + core
    other = 1 - core
    rows = 32
    half = 16
    depth = 128

    def dev(q):
        q = jnp.clip(q, 0, n - 1)
        return {"wide": q // 2, "narrow": q % 2}

    barrier = pltpu.get_barrier_semaphore()

    def greet(d, _):
        q = lax.rem(p + d, n)
        pl.semaphore_signal(barrier, inc=1, device_id={"wide": q // 2, "narrow": q % 2}, device_id_type=MESH)
        return 0

    lax.fori_loop(1, n, greet, 0)

    counter = [0]

    def remote(src, dst, target):
        i = counter[0]
        counter[0] += 1
        return pltpu.make_async_remote_copy(src_ref=src, dst_ref=dst, send_sem=send_sem.at[i], recv_sem=recv_sem.at[i],
                                            device_id=target, device_id_type=MESH)

    has = {-1: p >= 1, 1: p <= n - 2, -2: p >= 2, 2: p <= n - 3}
    chip = {-1: wide >= 1, 1: wide <= n_wide - 2}

    class Halo:
        def __init__(self, moves):
            self.moves = [(off, remote(src, dst, dev(p + off))) for off, src, dst in moves]

        def start(self):
            for off, copy in self.moves:
                pl.when(has[off])(copy.start)

        def recv(self):
            for off, copy in self.moves:
                pl.when(has[-off])(copy.wait_recv)

        def sent(self):
            for off, copy in self.moves:
                pl.when(has[off])(copy.wait_send)

    zf = jnp.zeros((4, rows, depth), f32)
    zc = jnp.zeros((rows, depth), f32)

    @pl.when(p == 0)
    def _():
        for l in (0, 1):
            k_r[l] = zf
            s_r[l] = zf
            c_r[l] = zf
            for cyc in (0, 1):
                b_r[cyc, l] = zf
                x1_r[cyc, l] = zf
                x2_r[cyc, l] = zf
            adj[l] = zf
        for l in (0, 1, 2):
            kc[l] = zc
            for cyc in (0, 1):
                g_r[cyc, l] = zc
                y2_r[cyc, l] = zc

    @pl.when(p == n - 1)
    def _():
        for l in (6, 7):
            k_r[l] = zf
            s_r[l] = zf
            c_r[l] = zf
            for cyc in (0, 1):
                b_r[cyc, l] = zf
                x1_r[cyc, l] = zf
                x2_r[cyc, l] = zf
            adj[l] = zf
        for l in (5, 6, 7):
            kc[l] = zc
            for cyc in (0, 1):
                g_r[cyc, l] = zc
                y2_r[cyc, l] = zc

    @pl.when(p == 1)
    def _():
        kc[0] = zc
        for cyc in (0, 1):
            y2_r[cyc, 0] = zc

    @pl.when(p == n - 2)
    def _():
        kc[7] = zc
        for cyc in (0, 1):
            y2_r[cyc, 7] = zc

    row_i = lax.broadcasted_iota(jnp.int32, (256, 256), 0)
    col_i = lax.broadcasted_iota(jnp.int32, (256, 256), 1)
    apart = jnp.where(row_i == jnp.where(col_i < 128, 2 * col_i, 2 * col_i - 255), 1.0, 0.0).astype(bf16)
    together = jnp.where(col_i == jnp.where(row_i < 128, 2 * row_i, 2 * row_i - 255), 1.0, 0.0).astype(bf16)

    mine = pl.multiple_of(half * core, half)
    theirs = pl.multiple_of(half * other, half)

    def planes(values, t_ref, region):
        flat = permuted(values.reshape(256, 256), apart)
        stage[0] = flat[:, :128].reshape(8, 32, 128)
        stage[1] = flat[:, 128:].reshape(8, 32, 128)
        for yp in range(2):
            for zp in range(2):
                t_ref[:, 2 * yp + zp] = stage[zp, :, pl.ds(yp, half, stride=2), :]
        region[pl.ds(2 - 2 * core, 6), :, pl.ds(mine, half), :] = t_ref[pl.ds(2 * core, 6)]

    planes(k_in[...], t_k, k_r)
    planes(k_in[...] * dir_in[...], t_c, c_r)
    planes(state_in[...], t_s, s_r)

    def first(t_ref, region, deep):
        i = counter[0]
        counter[0] += 6
        partner = pltpu.make_async_remote_copy(
            src_ref=t_ref.at[pl.ds(2 * other, 6)], dst_ref=region.at[pl.ds(2 - 2 * other, 6), :, pl.ds(mine, half), :],
            send_sem=send_sem.at[i], recv_sem=recv_sem.at[i], device_id={"narrow": other}, device_id_type=MESH)
        left = right = None
        if deep:
            left = pltpu.make_async_remote_copy(
                src_ref=t_ref.at[pl.ds(0, deep)], dst_ref=region.at[pl.ds(6, deep), :, pl.ds(mine, half), :],
                send_sem=send_sem.at[i + 1], recv_sem=recv_sem.at[i + 2 + core],
                device_id={"wide": jnp.maximum(wide - 1, 0), "narrow": 1}, device_id_type=MESH)
            right = pltpu.make_async_remote_copy(
                src_ref=t_ref.at[pl.ds(8 - deep, deep)], dst_ref=region.at[pl.ds(2 - deep, deep), :, pl.ds(mine, half), :],
                send_sem=send_sem.at[i + 2], recv_sem=recv_sem.at[i + 2 + core],
                device_id={"wide": jnp.minimum(wide + 1, n_wide - 1), "narrow": 0}, device_id_type=MESH)

        def start():
            if deep:
                pl.when(chip[-1])(left.start)
                pl.when(chip[1])(right.start)
            partner.start()

        def recv():
            partner.wait_recv()
            if deep:
                arrives = ((core == 0) & chip[-1]) | ((core == 1) & chip[1])

                @pl.when(arrives)
                def _():
                    for c in (0, 1):
                        at = jnp.where(core == 0, 2 - deep, 6)
                        pltpu.make_async_copy(t_ref.at[pl.ds(0, deep)],
                                              region.at[pl.ds(at, deep), :, pl.ds(half * c, half), :],
                                              recv_sem.at[i + 2 + c]).wait()

        def sent():
            partner.wait_send()
            if deep:
                pl.when(chip[-1])(left.wait_send)
                pl.when(chip[1])(right.wait_send)

        return start, recv, sent

    firsts = [first(t_k, k_r, 2), first(t_c, c_r, 1), first(t_s, s_r, 1)]
    weight_move = first(t_w, w_r, 0)

    pl.semaphore_wait(barrier, n - 1)
    for move in firsts:
        move[0]()
    planes(w_in[...], t_w, w_r)
    weight_move[0]()

    lane_i = lax.broadcasted_iota(jnp.int32, (rows, depth), 1)
    sub_i = lax.broadcasted_iota(jnp.int32, (rows, depth), 0)
    lane_first, lane_last = lane_i == 0, lane_i == depth - 1
    sub_first, sub_last = sub_i == 0, sub_i == rows - 1

    def after(v, axis):
        return pltpu.roll(v, v.shape[axis] - 1, axis)

    def before(v, axis):
        return pltpu.roll(v, 1, axis)

    def after0(v, axis):
        return jnp.where(sub_last if axis == 0 else lane_last, 0.0, after(v, axis))

    def before0(v, axis):
        return jnp.where(sub_first if axis == 0 else lane_first, 0.0, before(v, axis))

    pairs = ((1, ((0, 1), (2, 3))), (0, ((0, 2), (1, 3))))

    def four(ref, *index):
        return [ref[(*index, q)] for q in range(4)]

    def faces(c):
        inner, outer, around = {}, {}, [None] * 4
        for axis, sets in pairs:
            inner[axis], outer[axis] = [], []
            last = sub_last if axis == 0 else lane_last
            for ev, od in sets:
                inner[axis].append(0.5 * (c[ev] + c[od]))
                outer[axis].append(jnp.where(last, 0.0, 0.5 * (c[od] + after(c[ev], axis))))
                se = c[od] + before0(c[od], axis)
                so = c[ev] + after0(c[ev], axis)
                around[ev] = se if around[ev] is None else around[ev] + se
                around[od] = so if around[od] is None else around[od] + so
        return inner, outer, around

    def within(v, inner, outer):
        acc = [None] * 4
        for axis, sets in pairs:
            for i, (ev, od) in enumerate(sets):
                fi, fo = inner[axis][i], outer[axis][i]
                se = fi * v[od] + before(fo * v[od], axis)
                so = fi * v[ev] + fo * after(v[ev], axis)
                acc[ev] = se if acc[ev] is None else acc[ev] + se
                acc[od] = so if acc[od] is None else acc[od] + so
        return acc

    def loop(low, high, body):
        def step(l, _):
            body(l)
            return 0

        lax.fori_loop(low, high, step, 0)

    def cross(l):
        for q in range(4):
            cx[l, q] = 0.5 * (k_r[l, q] + k_r[l + 1, q])

    def prepare(l):
        c = four(k_r, l)
        inner, outer, around = faces(c)
        for i in range(2):
            czi[l, i], czo[l, i] = inner[1][i], outer[1][i]
            cyi[l, i], cyo[l, i] = inner[0][i], outer[0][i]
        layer = 4 * p - 2 + l
        inside = (layer >= 0) & (layer < 4 * n)
        for q in range(4):
            d = 3.0 * c[q] + 0.5 * (around[q] + k_r[l - 1, q] + k_r[l + 1, q])
            dia[l, q] = d
            inv[l, q] = jnp.where(inside, 1.0 / jnp.where(inside, d, 1.0), 0.0)

    def applied(ref, l, *index):
        v = four(ref, *index, l)
        inner = {1: [czi[l, 0], czi[l, 1]], 0: [cyi[l, 0], cyi[l, 1]]}
        outer = {1: [czo[l, 0], czo[l, 1]], 0: [cyo[l, 0], cyo[l, 1]]}
        acc = within(v, inner, outer)
        out = []
        for q in range(4):
            beside = acc[q] + (cx[l, q] * ref[(*index, l + 1, q)] + cx[l - 1, q] * ref[(*index, l - 1, q)])
            out.append(dia[l, q] * v[q] - beside)
        return out

    def source(l):
        c = four(c_r, l)
        inner, outer, around = faces(c)
        v = four(s_r, l)
        acc = within(v, inner, outer)
        for q in range(4):
            up, down = c_r[l + 1, q], c_r[l - 1, q]
            d = 3.0 * c[q] + 0.5 * (around[q] + up + down)
            beside = acc[q] + 0.5 * ((c[q] + up) * s_r[l + 1, q] + (c[q] + down) * s_r[l - 1, q])
            b_r[0, l, q] = beside - d * v[q]

    def start_smooth(l, cyc):
        for q in range(4):
            x1_r[cyc, l, q] = inv[l, q] * b_r[cyc, l, q] * inv_mid

    def end_smooth(l, cyc):
        ax = applied(x1_r, l, cyc)
        for q in range(4):
            x1 = x1_r[cyc, l, q]
            x2_r[cyc, l, q] = x1 + (carry_gain * x1 + step_gain * inv[l, q] * (b_r[cyc, l, q] - ax[q]))

    def whole_sum(v):
        return jnp.sum(jnp.sum(v, axis=0, keepdims=True), axis=1, keepdims=True)

    def coarse_prepare(l):
        c = kc[l]
        up, down = kc[l + 1], kc[l - 1]
        ccy[l] = jnp.where(sub_last, 0.0, 0.125 * (c + after(c, 0)))
        ccz[l] = jnp.where(lane_last, 0.0, 0.125 * (c + after(c, 1)))
        around = after0(c, 0) + before0(c, 0) + after0(c, 1) + before0(c, 1) + up + down
        d = 0.25 * (3.0 * c + 0.5 * around)
        layer = 2 * p - 3 + l
        inside = (layer >= 0) & (layer < 2 * n)
        diac[l] = d
        invc[l] = jnp.where(inside, 1.0 / jnp.where(inside, d, 1.0), 0.0)

    def coarse_cross(l):
        ccx[l] = 0.125 * (kc[l] + kc[l + 1])

    def coarse_applied(get, l):
        v = get(l)
        fy, fz = ccy[l], ccz[l]
        beside = fy * after(v, 0) + before(fy * v, 0) + fz * after(v, 1) + before(fz * v, 1)
        beside = beside + (ccx[l] * get(l + 1) + ccx[l - 1] * get(l - 1))
        return diac[l] * v - beside

    def home(o_ref, t_ref):
        return remote(o_ref.at[:, :, pl.ds(theirs, half), :], t_ref.at[pl.ds(4 * core, 4)], {"narrow": other})

    def assemble(o_ref, t_ref, out_ref):
        t_ref[pl.ds(4 * core, 4)] = o_ref[:, :, pl.ds(mine, half), :]
        for yp in range(2):
            for zp in range(2):
                stage[zp, :, pl.ds(yp, half, stride=2), :] = t_ref[:, 2 * yp + zp]
        flat = jnp.concatenate([stage[0].reshape(256, 128), stage[1].reshape(256, 128)], axis=1)
        out_ref[...] = permuted(flat, together).reshape(8, 32, 256)

    for move in firsts:
        move[1]()

    for j in (0, 1):
        total = None
        for l in (2 + 2 * j, 3 + 2 * j):
            for q in range(4):
                total = k_r[l, q] if total is None else total + k_r[l, q]
        kc[3 + j] = 0.125 * total
    halo_kc = Halo([(-1, kc.at[pl.ds(3, 2)], kc.at[pl.ds(5, 2)]), (1, kc.at[pl.ds(3, 2)], kc.at[pl.ds(1, 2)]),
                    (-2, kc.at[3], kc.at[7]), (2, kc.at[4], kc.at[0])])
    pending = []

    loop(2, 6, prepare)
    loop(2, 6, source)
    half_row = sub_i < half

    for cyc in (0, 1):
        if cyc == 1:
            def adjoint_source(l):
                for q in range(4):
                    b_r[1, l, q] = -(w_r[l, q] * o_inc[l - 2, q])

            weight_move[1]()
            loop(2, 6, adjoint_source)
        loop(2, 6, functools.partial(start_smooth, cyc=cyc))
        halo_b = Halo([(-1, b_r.at[cyc, 2], b_r.at[cyc, 6]), (1, b_r.at[cyc, 5], b_r.at[cyc, 1]),
                       (-1, x1_r.at[cyc, 3], x1_r.at[cyc, 7]), (1, x1_r.at[cyc, 4], x1_r.at[cyc, 0])])
        halo_b.start()
        pending.append(halo_b)
        if cyc == 0:
            halo_kc.start()
            pending.append(halo_kc)
            loop(0, 7, cross)
            prepare(1)
            prepare(6)
        else:
            inc_move = home(o_inc, r_inc)
            inc_move.start()
        loop(3, 5, functools.partial(end_smooth, cyc=cyc))
        halo_b.recv()
        start_smooth(1, cyc)
        start_smooth(6, cyc)
        loop(1, 3, functools.partial(end_smooth, cyc=cyc))
        loop(5, 7, functools.partial(end_smooth, cyc=cyc))
        halo_x2 = Halo([(-1, x2_r.at[cyc, 3], x2_r.at[cyc, 7]), (1, x2_r.at[cyc, 4], x2_r.at[cyc, 0])])

        def restrict(j):
            total = None
            for i in (0, 1):
                l = 2 * j - 4 + i
                ax = applied(x2_r, l, cyc)
                for q in range(4):
                    r = b_r[cyc, l, q] - ax[q]
                    total = r if total is None else total + r
            g_r[cyc, j] = 0.125 * total

        loop(3, 5, restrict)
        halo_g = Halo([(-1, g_r.at[cyc, pl.ds(3, 2)], g_r.at[cyc, pl.ds(5, 2)]),
                       (1, g_r.at[cyc, pl.ds(3, 2)], g_r.at[cyc, pl.ds(1, 2)])])
        halo_g.start()
        halo_x2.start()
        pending += [halo_g, halo_x2]
        if cyc == 0:
            halo_kc.recv()
            loop(0, 7, coarse_cross)
            loop(1, 7, coarse_prepare)
        else:
            inc_move.wait_recv()
            assemble(o_inc, r_inc, inc_out)
        halo_g.recv()

        def coarse_start(l):
            y1[l] = invc[l] * g_r[cyc, l] * inv_mid

        def coarse_end(l):
            ay = coarse_applied(lambda i: y1[i], l)
            v = y1[l]
            y2_r[cyc, l] = v + (carry_gain * v + step_gain * invc[l] * (g_r[cyc, l] - ay))

        loop(1, 7, coarse_start)
        loop(2, 6, coarse_end)
        halo_y = Halo([(-1, y2_r.at[cyc, 4], y2_r.at[cyc, 6]), (1, y2_r.at[cyc, 3], y2_r.at[cyc, 1]),
                       (-2, y2_r.at[cyc, 3], y2_r.at[cyc, 7]), (2, y2_r.at[cyc, 4], y2_r.at[cyc, 0])])
        left_over = None
        for l in (3, 4):
            r = g_r[cyc, l] - coarse_applied(lambda i: y2_r[cyc, i], l)
            left_over = r if left_over is None else left_over + r
        low = whole_sum(left_over[:half])
        high = whole_sum(left_over[half:])
        slots = lax.broadcasted_iota(jnp.int32, (1, tot.shape[-1]), 1)
        tot[cyc, 0] = jnp.where(slots == 2 * wide, low, jnp.where(slots == 2 * wide + 1, high, 0.0))
        sem_at = counter[0]
        counter[0] += 1

        def total_copy(d):
            q = lax.rem(p + d, n)
            return pltpu.make_async_remote_copy(
                src_ref=tot.at[cyc, 0], dst_ref=tot.at[cyc, d], send_sem=send_sem.at[sem_at],
                recv_sem=recv_sem.at[sem_at], device_id={"wide": q // 2, "narrow": q % 2}, device_id_type=MESH)

        loop(1, n, lambda d: total_copy(d).start())
        halo_y.start()
        pending.append(halo_y)
        halo_y.recv()
        everyone = tot.at[cyc, pl.ds(1, n - 1)]
        pltpu.make_async_copy(everyone, everyone, recv_sem.at[sem_at]).wait()
        pltpu.make_async_copy(everyone, everyone, send_sem.at[sem_at]).wait()
        totals = jnp.sum(tot[cyc], axis=0)[:, :nb]
        for i in range(3):
            at = jnp.clip(wide + i - 1, 0, n_wide - 1)
            ends = wide + i - 1
            inside = (ends >= 0) & (ends < n_wide)
            values = []
            for h in range(2):
                row = inv_in[pl.ds(2 * at + h, 1), :]
                values.append(jnp.sum(row * totals, axis=1, keepdims=True))
            corr[i] = jnp.where(inside, jnp.where(half_row, values[0], values[1]), 0.0)

        def coarse_add(l):
            ya[l] = y2_r[cyc, l] + corr[(2 * core + 1 + l) // 4]

        def coarse_third(l):
            e = invc[l] * (g_r[cyc, l] - coarse_applied(lambda i: ya[i], l)) * inv_mid
            updc[l] = e
            yb[l] = ya[l] + e

        def coarse_fourth(l):
            r = g_r[cyc, l] - coarse_applied(lambda i: yb[i], l)
            y1[l] = yb[l] + (carry_gain * updc[l] + step_gain * invc[l] * r)

        loop(0, 8, coarse_add)
        loop(1, 7, coarse_third)
        loop(2, 6, coarse_fourth)
        halo_x2.recv()

        def prolong(j):
            y = y1[j]
            for i in (0, 1):
                l = 2 * j - 4 + i
                for q in range(4):
                    xa[l, q] = x2_r[cyc, l, q] + y

        def third(l):
            ax = applied(xa, l)
            for q in range(4):
                e = inv[l, q] * (b_r[cyc, l, q] - ax[q]) * inv_mid
                upd[l, q] = e
                xb[l, q] = xa[l, q] + e

        def fourth(l):
            ax = applied(xb, l)
            for q in range(4):
                r = b_r[cyc, l, q] - ax[q]
                out = xb[l, q] + (carry_gain * upd[l, q] + step_gain * inv[l, q] * r)
                if cyc == 0:
                    o_inc[l - 2, q] = out
                else:
                    adj[l, q] = out

        loop(2, 6, prolong)
        loop(1, 7, third)
        loop(2, 6, fourth)

    halo_adj = Halo([(-1, adj.at[2], adj.at[6]), (1, adj.at[5], adj.at[1])])
    halo_adj.start()
    pending.append(halo_adj)

    def hessian(l):
        s, a = four(s_r, l), four(adj, l)
        acc = [(s[q] - s_r[l + 1, q]) * (a[q] - adj[l + 1, q]) + (s[q] - s_r[l - 1, q]) * (a[q] - adj[l - 1, q])
               for q in range(4)]
        for axis, sets in pairs:
            first_one = sub_first if axis == 0 else lane_first
            for ev, od in sets:
                i = (s[ev] - s[od]) * (a[ev] - a[od])
                o = (s[od] - after0(s[ev], axis)) * (a[od] - after0(a[ev], axis))
                acc[ev] = acc[ev] + i + jnp.where(first_one, s[ev] * a[ev], before(o, axis))
                acc[od] = acc[od] + i + o
        for q in range(4):
            o_hess[l - 2, q] = 0.5 * k_r[l, q] * acc[q]

    loop(3, 5, hessian)
    halo_adj.recv()
    hessian(2)
    hessian(5)

    hess_move = home(o_hess, r_hess)
    hess_move.start()
    hess_move.wait_recv()
    assemble(o_hess, r_hess, hess_out)
    for halo in pending:
        halo.sent()
    for move in firsts + [weight_move]:
        move[2]()
    inc_move.wait_send()
    hess_move.wait_send()


def shards(n, state, permeability, direction, obs_weight, coarse_inverse):
    nb = coarse_inverse.shape[0]
    width = max(128, nb)
    fine = pltpu.VMEM((8, 4, 32, 128), f32)
    fine2 = pltpu.VMEM((2, 8, 4, 32, 128), f32)
    face = pltpu.VMEM((8, 2, 32, 128), f32)
    turned = pltpu.VMEM((8, 4, 16, 128), f32)
    coarse = pltpu.VMEM((8, 32, 128), f32)
    coarse2 = pltpu.VMEM((2, 8, 32, 128), f32)
    owned = pltpu.VMEM((4, 4, 32, 128), f32)
    vmem = pl.BlockSpec(memory_space=pltpu.VMEM)
    scratch = [pltpu.VMEM((2, 8, 32, 128), f32)] + [turned] * 4 + [fine] * 4 + [face] * 4 + [fine] * 3
    scratch += [fine2] * 3 + [fine] * 3
    scratch += [coarse] * 6 + [coarse2, coarse, coarse2] + [coarse] * 3
    scratch += [pltpu.VMEM((2, n, 1, width), f32), pltpu.VMEM((3, 32, 128), f32), fine, owned, owned, turned, turned]
    scratch += [pltpu.SemaphoreType.DMA((72,)), pltpu.SemaphoreType.DMA((72,))]
    shape = jax.ShapeDtypeStruct(state.shape, f32)
    return pl.pallas_call(
        functools.partial(kernel, n, nb),
        out_shape=(shape, shape),
        in_specs=[vmem] * 5,
        out_specs=(vmem, vmem),
        scratch_shapes=scratch,
        compiler_params=pltpu.CompilerParams(collective_id=0, has_side_effects=True, vmem_limit_bytes=40 * 1024 * 1024),
    )(state, permeability, direction, obs_weight, coarse_inverse)


def solution(mesh):
    field = P(("parts", "wide"), "narrow", None)
    return jax.shard_map(
        functools.partial(shards, mesh.shape["wide"] * mesh.shape["narrow"]),
        mesh=mesh,
        in_specs=(field, field, field, field, P("parts", None)),
        out_specs=(field, field),
        check_vma=False,
    )
```

```python
import functools

import jax
import jax.numpy as jnp
from jax import lax
from jax.experimental import pallas as pl
from jax.experimental.pallas import tpu as pltpu
from jax.sharding import PartitionSpec as P

MESH = pl.DeviceIdType.MESH
f32 = jnp.float32
bf16 = jnp.bfloat16

cheb_mid = 1.125
cheb_half = 0.875
first_rho = cheb_half / cheb_mid
second_rho = 1.0 / (2.0 * cheb_mid / cheb_half - first_rho)
step_gain = 2.0 * second_rho / cheb_half
carry_gain = second_rho * first_rho
inv_mid = 1.0 / cheb_mid


def split3(a):
    hi = a.astype(bf16)
    rest = a - hi.astype(f32)
    mid = rest.astype(bf16)
    low = (rest - mid.astype(f32)).astype(bf16)
    return hi, mid, low


def permuted(a, perm):
    parts = [jnp.dot(s, perm, preferred_element_type=f32) for s in split3(a)]
    return parts[0] + (parts[1] + parts[2])


def kernel(n, nb, state_hbm, k_hbm, dir_hbm, w_hbm, inv_hbm, hess_out, inc_out, state_in, k_in, dir_in, w_in, inv_in, stage, t_s, t_k, t_c, t_w, s_r, k_r, c_r, w_r,
           czi, czo, cyi, cyo, cx, dia, inv, b_r, x1_r, x2_r, xa, xb, upd, kc, ccx, ccy, ccz, diac, invc, g_r, y1, y2_r,
           ya, yb, updc, tot, corr, adj, o_inc, o_hess, r_inc, r_hess, send_sem, recv_sem, load_sem):
    wide = lax.axis_index("wide")
    core = lax.axis_index("narrow")
    n_wide = n // 2
    p = 2 * wide + core
    other = 1 - core
    rows = 32
    half = 16
    depth = 128

    def dev(q):
        q = jnp.clip(q, 0, n - 1)
        return {"wide": q // 2, "narrow": q % 2}

    sources = (k_hbm, dir_hbm, state_hbm, w_hbm, inv_hbm)
    loads = [pltpu.make_async_copy(src, dst, load_sem.at[i])
             for i, (src, dst) in enumerate(zip(sources, (k_in, dir_in, state_in, w_in, inv_in)))]
    for load in loads:
        load.start()

    barrier = pltpu.get_barrier_semaphore()

    def greet(d, _):
        q = lax.rem(p + d, n)
        pl.semaphore_signal(barrier, inc=1, device_id={"wide": q // 2, "narrow": q % 2}, device_id_type=MESH)
        return 0

    lax.fori_loop(1, n, greet, 0)

    counter = [0]

    def remote(src, dst, target):
        i = counter[0]
        counter[0] += 1
        return pltpu.make_async_remote_copy(src_ref=src, dst_ref=dst, send_sem=send_sem.at[i], recv_sem=recv_sem.at[i],
                                            device_id=target, device_id_type=MESH)

    has = {-1: p >= 1, 1: p <= n - 2, -2: p >= 2, 2: p <= n - 3}
    chip = {-1: wide >= 1, 1: wide <= n_wide - 2}

    class Halo:
        def __init__(self, moves):
            self.moves = [(off, remote(src, dst, dev(p + off))) for off, src, dst in moves]

        def start(self):
            for off, copy in self.moves:
                pl.when(has[off])(copy.start)

        def recv(self):
            for off, copy in self.moves:
                pl.when(has[-off])(copy.wait_recv)

        def sent(self):
            for off, copy in self.moves:
                pl.when(has[off])(copy.wait_send)

    zf = jnp.zeros((4, rows, depth), f32)
    zc = jnp.zeros((rows, depth), f32)

    @pl.when(p == 0)
    def _():
        for l in (0, 1):
            k_r[l] = zf
            s_r[l] = zf
            c_r[l] = zf
            for cyc in (0, 1):
                b_r[cyc, l] = zf
                x1_r[cyc, l] = zf
                x2_r[cyc, l] = zf
            adj[l] = zf
        for l in (0, 1, 2):
            kc[l] = zc
            for cyc in (0, 1):
                g_r[cyc, l] = zc
                y2_r[cyc, l] = zc

    @pl.when(p == n - 1)
    def _():
        for l in (6, 7):
            k_r[l] = zf
            s_r[l] = zf
            c_r[l] = zf
            for cyc in (0, 1):
                b_r[cyc, l] = zf
                x1_r[cyc, l] = zf
                x2_r[cyc, l] = zf
            adj[l] = zf
        for l in (5, 6, 7):
            kc[l] = zc
            for cyc in (0, 1):
                g_r[cyc, l] = zc
                y2_r[cyc, l] = zc

    @pl.when(p == 1)
    def _():
        kc[0] = zc
        for cyc in (0, 1):
            y2_r[cyc, 0] = zc

    @pl.when(p == n - 2)
    def _():
        kc[7] = zc
        for cyc in (0, 1):
            y2_r[cyc, 7] = zc

    row_i = lax.broadcasted_iota(jnp.int32, (256, 256), 0)
    col_i = lax.broadcasted_iota(jnp.int32, (256, 256), 1)
    apart = jnp.where(row_i == jnp.where(col_i < 128, 2 * col_i, 2 * col_i - 255), 1.0, 0.0).astype(bf16)
    together = jnp.where(col_i == jnp.where(row_i < 128, 2 * row_i, 2 * row_i - 255), 1.0, 0.0).astype(bf16)

    mine = pl.multiple_of(half * core, half)
    theirs = pl.multiple_of(half * other, half)

    def planes(values, t_ref, region):
        flat = permuted(values.reshape(256, 256), apart)
        stage[0] = flat[:, :128].reshape(8, 32, 128)
        stage[1] = flat[:, 128:].reshape(8, 32, 128)
        for yp in range(2):
            for zp in range(2):
                t_ref[:, 2 * yp + zp] = stage[zp, :, pl.ds(yp, half, stride=2), :]
        region[pl.ds(2 - 2 * core, 6), :, pl.ds(mine, half), :] = t_ref[pl.ds(2 * core, 6)]

    loads[0].wait()
    planes(k_in[...], t_k, k_r)
    loads[1].wait()
    planes(k_in[...] * dir_in[...], t_c, c_r)
    loads[2].wait()
    planes(state_in[...], t_s, s_r)

    def first(t_ref, region, deep, skip=0):
        i = counter[0]
        counter[0] += 6
        partner = pltpu.make_async_remote_copy(
            src_ref=t_ref.at[pl.ds(2 * other, 6)], dst_ref=region.at[pl.ds(2 - 2 * other, 6), :, pl.ds(mine, half), :],
            send_sem=send_sem.at[i], recv_sem=recv_sem.at[i], device_id={"narrow": other}, device_id_type=MESH)
        left = right = None
        if deep:
            left = pltpu.make_async_remote_copy(
                src_ref=t_ref.at[pl.ds(skip, deep)], dst_ref=region.at[pl.ds(6 + skip, deep), :, pl.ds(mine, half), :],
                send_sem=send_sem.at[i + 1], recv_sem=recv_sem.at[i + 2 + core],
                device_id={"wide": jnp.maximum(wide - 1, 0), "narrow": 1}, device_id_type=MESH)
            right = pltpu.make_async_remote_copy(
                src_ref=t_ref.at[pl.ds(8 - skip - deep, deep)], dst_ref=region.at[pl.ds(2 - skip - deep, deep), :, pl.ds(mine, half), :],
                send_sem=send_sem.at[i + 2], recv_sem=recv_sem.at[i + 2 + core],
                device_id={"wide": jnp.minimum(wide + 1, n_wide - 1), "narrow": 0}, device_id_type=MESH)

        def start():
            if deep:
                pl.when(chip[-1])(left.start)
                pl.when(chip[1])(right.start)
            if not skip:
                partner.start()

        def recv():
            if not skip:
                partner.wait_recv()
            if deep:
                arrives = ((core == 0) & chip[-1]) | ((core == 1) & chip[1])

                @pl.when(arrives)
                def _():
                    for c in (0, 1):
                        at = jnp.where(core == 0, 2 - skip - deep, 6 + skip)
                        pltpu.make_async_copy(t_ref.at[pl.ds(0, deep)],
                                              region.at[pl.ds(at, deep), :, pl.ds(half * c, half), :],
                                              recv_sem.at[i + 2 + c]).wait()

        def sent():
            if not skip:
                partner.wait_send()
            if deep:
                pl.when(chip[-1])(left.wait_send)
                pl.when(chip[1])(right.wait_send)

        return start, recv, sent

    firsts = [first(t_k, k_r, 1), first(t_c, c_r, 1), first(t_s, s_r, 1)]
    weight_move = first(t_w, w_r, 0)
    second_k = first(t_k, k_r, 1, 1)

    pl.semaphore_wait(barrier, n - 1)
    for move in firsts:
        move[0]()
    loads[3].wait()
    loads[4].wait()
    planes(w_in[...], t_w, w_r)
    weight_move[0]()

    lane_i = lax.broadcasted_iota(jnp.int32, (rows, depth), 1)
    sub_i = lax.broadcasted_iota(jnp.int32, (rows, depth), 0)
    lane_first, lane_last = lane_i == 0, lane_i == depth - 1
    sub_first, sub_last = sub_i == 0, sub_i == rows - 1

    def after(v, axis):
        return pltpu.roll(v, v.shape[axis] - 1, axis)

    def before(v, axis):
        return pltpu.roll(v, 1, axis)

    def after0(v, axis):
        return jnp.where(sub_last if axis == 0 else lane_last, 0.0, after(v, axis))

    def before0(v, axis):
        return jnp.where(sub_first if axis == 0 else lane_first, 0.0, before(v, axis))

    pairs = ((1, ((0, 1), (2, 3))), (0, ((0, 2), (1, 3))))

    def four(ref, *index):
        return [ref[(*index, q)] for q in range(4)]

    def faces(c):
        inner, outer, around = {}, {}, [None] * 4
        for axis, sets in pairs:
            inner[axis], outer[axis] = [], []
            last = sub_last if axis == 0 else lane_last
            for ev, od in sets:
                inner[axis].append(0.5 * (c[ev] + c[od]))
                outer[axis].append(jnp.where(last, 0.0, 0.5 * (c[od] + after(c[ev], axis))))
                se = c[od] + before0(c[od], axis)
                so = c[ev] + after0(c[ev], axis)
                around[ev] = se if around[ev] is None else around[ev] + se
                around[od] = so if around[od] is None else around[od] + so
        return inner, outer, around

    def within(v, inner, outer):
        acc = [None] * 4
        for axis, sets in pairs:
            for i, (ev, od) in enumerate(sets):
                fi, fo = inner[axis][i], outer[axis][i]
                se = fi * v[od] + before(fo * v[od], axis)
                so = fi * v[ev] + fo * after(v[ev], axis)
                acc[ev] = se if acc[ev] is None else acc[ev] + se
                acc[od] = so if acc[od] is None else acc[od] + so
        return acc

    def loop(low, high, body):
        def step(l, _):
            body(l)
            return 0

        lax.fori_loop(low, high, step, 0)

    def cross(l):
        for q in range(4):
            cx[l, q] = 0.5 * (k_r[l, q] + k_r[l + 1, q])

    def prepare(l):
        c = four(k_r, l)
        inner, outer, around = faces(c)
        for i in range(2):
            czi[l, i], czo[l, i] = inner[1][i], outer[1][i]
            cyi[l, i], cyo[l, i] = inner[0][i], outer[0][i]
        layer = 4 * p - 2 + l
        inside = (layer >= 0) & (layer < 4 * n)
        for q in range(4):
            d = 3.0 * c[q] + 0.5 * (around[q] + k_r[l - 1, q] + k_r[l + 1, q])
            dia[l, q] = d
            inv[l, q] = jnp.where(inside, 1.0 / jnp.where(inside, d, 1.0), 0.0)

    def applied(ref, l, *index):
        v = four(ref, *index, l)
        inner = {1: [czi[l, 0], czi[l, 1]], 0: [cyi[l, 0], cyi[l, 1]]}
        outer = {1: [czo[l, 0], czo[l, 1]], 0: [cyo[l, 0], cyo[l, 1]]}
        acc = within(v, inner, outer)
        out = []
        for q in range(4):
            beside = acc[q] + (cx[l, q] * ref[(*index, l + 1, q)] + cx[l - 1, q] * ref[(*index, l - 1, q)])
            out.append(dia[l, q] * v[q] - beside)
        return out

    def source(l):
        c = four(c_r, l)
        inner, outer, around = faces(c)
        v = four(s_r, l)
        acc = within(v, inner, outer)
        for q in range(4):
            up, down = c_r[l + 1, q], c_r[l - 1, q]
            d = 3.0 * c[q] + 0.5 * (around[q] + up + down)
            beside = acc[q] + 0.5 * ((c[q] + up) * s_r[l + 1, q] + (c[q] + down) * s_r[l - 1, q])
            b_r[0, l, q] = beside - d * v[q]

    def start_smooth(l, cyc):
        for q in range(4):
            x1_r[cyc, l, q] = inv[l, q] * b_r[cyc, l, q] * inv_mid

    def end_smooth(l, cyc):
        ax = applied(x1_r, l, cyc)
        for q in range(4):
            x1 = x1_r[cyc, l, q]
            x2_r[cyc, l, q] = x1 + (carry_gain * x1 + step_gain * inv[l, q] * (b_r[cyc, l, q] - ax[q]))

    def whole_sum(v):
        return jnp.sum(jnp.sum(v, axis=0, keepdims=True), axis=1, keepdims=True)

    def coarse_prepare(l):
        c = kc[l]
        up, down = kc[l + 1], kc[l - 1]
        ccy[l] = jnp.where(sub_last, 0.0, 0.125 * (c + after(c, 0)))
        ccz[l] = jnp.where(lane_last, 0.0, 0.125 * (c + after(c, 1)))
        around = after0(c, 0) + before0(c, 0) + after0(c, 1) + before0(c, 1) + up + down
        d = 0.25 * (3.0 * c + 0.5 * around)
        layer = 2 * p - 3 + l
        inside = (layer >= 0) & (layer < 2 * n)
        diac[l] = d
        invc[l] = jnp.where(inside, 1.0 / jnp.where(inside, d, 1.0), 0.0)

    def coarse_cross(l):
        ccx[l] = 0.125 * (kc[l] + kc[l + 1])

    def coarse_applied(get, l):
        v = get(l)
        fy, fz = ccy[l], ccz[l]
        beside = fy * after(v, 0) + before(fy * v, 0) + fz * after(v, 1) + before(fz * v, 1)
        beside = beside + (ccx[l] * get(l + 1) + ccx[l - 1] * get(l - 1))
        return diac[l] * v - beside

    def home(o_ref, t_ref):
        return remote(o_ref.at[:, :, pl.ds(theirs, half), :], t_ref.at[pl.ds(4 * core, 4)], {"narrow": other})

    def assemble(o_ref, t_ref, out_ref):
        t_ref[pl.ds(4 * core, 4)] = o_ref[:, :, pl.ds(mine, half), :]
        for yp in range(2):
            for zp in range(2):
                stage[zp, :, pl.ds(yp, half, stride=2), :] = t_ref[:, 2 * yp + zp]
        flat = jnp.concatenate([stage[0].reshape(256, 128), stage[1].reshape(256, 128)], axis=1)
        out_ref[...] = permuted(flat, together).reshape(8, 32, 256)

    for move in firsts:
        move[1]()

    for j in (0, 1):
        total = None
        for l in (2 + 2 * j, 3 + 2 * j):
            for q in range(4):
                total = k_r[l, q] if total is None else total + k_r[l, q]
        kc[3 + j] = 0.125 * total
    halo_kc = Halo([(-1, kc.at[pl.ds(3, 2)], kc.at[pl.ds(5, 2)]), (1, kc.at[pl.ds(3, 2)], kc.at[pl.ds(1, 2)]),
                    (-2, kc.at[3], kc.at[7]), (2, kc.at[4], kc.at[0])])
    second_k[0]()
    halo_kc.start()
    pending = [halo_kc]

    loop(2, 6, prepare)
    loop(2, 6, source)
    half_row = sub_i < half

    for cyc in (0, 1):
        if cyc == 1:
            def adjoint_source(l):
                for q in range(4):
                    b_r[1, l, q] = -(w_r[l, q] * o_inc[l - 2, q])

            weight_move[1]()
            loop(2, 6, adjoint_source)
        loop(2, 6, functools.partial(start_smooth, cyc=cyc))
        halo_b = Halo([(-1, b_r.at[cyc, 2], b_r.at[cyc, 6]), (1, b_r.at[cyc, 5], b_r.at[cyc, 1])])
        halo_x1 = Halo([(-1, x1_r.at[cyc, 3], x1_r.at[cyc, 7]), (1, x1_r.at[cyc, 4], x1_r.at[cyc, 0])])
        halo_b.start()
        halo_x1.start()
        pending += [halo_b, halo_x1]
        if cyc == 0:
            loop(1, 6, cross)
        else:
            inc_move = home(o_inc, r_inc)
            inc_move.start()
        loop(3, 5, functools.partial(end_smooth, cyc=cyc))
        if cyc == 0:
            second_k[1]()
            cross(0)
            cross(6)
            prepare(1)
            prepare(6)
        halo_b.recv()
        start_smooth(1, cyc)
        start_smooth(6, cyc)
        halo_x2 = Halo([(-1, x2_r.at[cyc, 3], x2_r.at[cyc, 7]), (1, x2_r.at[cyc, 4], x2_r.at[cyc, 0])])
        end_smooth(2, cyc)
        end_smooth(5, cyc)
        halo_x1.recv()
        halo_x2.start()
        end_smooth(1, cyc)
        end_smooth(6, cyc)

        def restrict(j):
            total = None
            for i in (0, 1):
                l = 2 * j - 4 + i
                ax = applied(x2_r, l, cyc)
                for q in range(4):
                    r = b_r[cyc, l, q] - ax[q]
                    total = r if total is None else total + r
            g_r[cyc, j] = 0.125 * total

        loop(3, 5, restrict)
        halo_g = Halo([(-1, g_r.at[cyc, pl.ds(3, 2)], g_r.at[cyc, pl.ds(5, 2)]),
                       (1, g_r.at[cyc, pl.ds(3, 2)], g_r.at[cyc, pl.ds(1, 2)])])
        halo_g.start()
        pending += [halo_g, halo_x2]
        if cyc == 0:
            halo_kc.recv()
            loop(0, 7, coarse_cross)
            loop(1, 7, coarse_prepare)
        else:
            inc_move.wait_recv()
            assemble(o_inc, r_inc, inc_out)
        halo_g.recv()

        def coarse_start(l):
            y1[l] = invc[l] * g_r[cyc, l] * inv_mid

        def coarse_end(l):
            ay = coarse_applied(lambda i: y1[i], l)
            v = y1[l]
            y2_r[cyc, l] = v + (carry_gain * v + step_gain * invc[l] * (g_r[cyc, l] - ay))

        loop(1, 7, coarse_start)
        loop(2, 6, coarse_end)
        halo_y = Halo([(-1, y2_r.at[cyc, 4], y2_r.at[cyc, 6]), (1, y2_r.at[cyc, 3], y2_r.at[cyc, 1]),
                       (-2, y2_r.at[cyc, 3], y2_r.at[cyc, 7]), (2, y2_r.at[cyc, 4], y2_r.at[cyc, 0])])
        left_over = None
        for l in (3, 4):
            r = g_r[cyc, l] - coarse_applied(lambda i: y2_r[cyc, i], l)
            left_over = r if left_over is None else left_over + r
        low = whole_sum(left_over[:half])
        high = whole_sum(left_over[half:])
        slots = lax.broadcasted_iota(jnp.int32, (1, tot.shape[-1]), 1)
        tot[cyc, 0] = jnp.where(slots == 2 * wide, low, jnp.where(slots == 2 * wide + 1, high, 0.0))
        sem_at = counter[0]
        counter[0] += 1

        def total_copy(d):
            q = lax.rem(p + d, n)
            return pltpu.make_async_remote_copy(
                src_ref=tot.at[cyc, 0], dst_ref=tot.at[cyc, d], send_sem=send_sem.at[sem_at],
                recv_sem=recv_sem.at[sem_at], device_id={"wide": q // 2, "narrow": q % 2}, device_id_type=MESH)

        loop(1, n, lambda d: total_copy(d).start())
        halo_y.start()
        pending.append(halo_y)
        halo_y.recv()
        everyone = tot.at[cyc, pl.ds(1, n - 1)]
        pltpu.make_async_copy(everyone, everyone, recv_sem.at[sem_at]).wait()
        pltpu.make_async_copy(everyone, everyone, send_sem.at[sem_at]).wait()
        totals = jnp.sum(tot[cyc], axis=0)[:, :nb]
        for i in range(3):
            at = jnp.clip(wide + i - 1, 0, n_wide - 1)
            ends = wide + i - 1
            inside = (ends >= 0) & (ends < n_wide)
            values = []
            for h in range(2):
                row = inv_in[pl.ds(2 * at + h, 1), :]
                values.append(jnp.sum(row * totals, axis=1, keepdims=True))
            corr[i] = jnp.where(inside, jnp.where(half_row, values[0], values[1]), 0.0)

        def coarse_add(l):
            ya[l] = y2_r[cyc, l] + corr[(2 * core + 1 + l) // 4]

        def coarse_third(l):
            e = invc[l] * (g_r[cyc, l] - coarse_applied(lambda i: ya[i], l)) * inv_mid
            updc[l] = e
            yb[l] = ya[l] + e

        def coarse_fourth(l):
            r = g_r[cyc, l] - coarse_applied(lambda i: yb[i], l)
            y1[l] = yb[l] + (carry_gain * updc[l] + step_gain * invc[l] * r)

        loop(0, 8, coarse_add)
        loop(1, 7, coarse_third)
        loop(2, 6, coarse_fourth)
        halo_x2.recv()

        def prolong(j):
            y = y1[j]
            for i in (0, 1):
                l = 2 * j - 4 + i
                for q in range(4):
                    xa[l, q] = x2_r[cyc, l, q] + y

        def third(l):
            ax = applied(xa, l)
            for q in range(4):
                e = inv[l, q] * (b_r[cyc, l, q] - ax[q]) * inv_mid
                upd[l, q] = e
                xb[l, q] = xa[l, q] + e

        def fourth(l):
            ax = applied(xb, l)
            for q in range(4):
                r = b_r[cyc, l, q] - ax[q]
                out = xb[l, q] + (carry_gain * upd[l, q] + step_gain * inv[l, q] * r)
                if cyc == 0:
                    o_inc[l - 2, q] = out
                else:
                    adj[l, q] = out

        loop(2, 6, prolong)
        loop(1, 7, third)
        loop(2, 6, fourth)

    halo_adj = Halo([(-1, adj.at[2], adj.at[6]), (1, adj.at[5], adj.at[1])])
    halo_adj.start()
    pending.append(halo_adj)

    def hessian(l):
        s, a = four(s_r, l), four(adj, l)
        acc = [(s[q] - s_r[l + 1, q]) * (a[q] - adj[l + 1, q]) + (s[q] - s_r[l - 1, q]) * (a[q] - adj[l - 1, q])
               for q in range(4)]
        for axis, sets in pairs:
            first_one = sub_first if axis == 0 else lane_first
            for ev, od in sets:
                i = (s[ev] - s[od]) * (a[ev] - a[od])
                o = (s[od] - after0(s[ev], axis)) * (a[od] - after0(a[ev], axis))
                acc[ev] = acc[ev] + i + jnp.where(first_one, s[ev] * a[ev], before(o, axis))
                acc[od] = acc[od] + i + o
        for q in range(4):
            o_hess[l - 2, q] = 0.5 * k_r[l, q] * acc[q]

    loop(3, 5, hessian)
    halo_adj.recv()
    hessian(2)
    hessian(5)

    hess_move = home(o_hess, r_hess)
    hess_move.start()
    hess_move.wait_recv()
    assemble(o_hess, r_hess, hess_out)
    for halo in pending:
        halo.sent()
    for move in firsts + [weight_move, second_k]:
        move[2]()
    inc_move.wait_send()
    hess_move.wait_send()


def shards(n, state, permeability, direction, obs_weight, coarse_inverse):
    nb = coarse_inverse.shape[0]
    width = max(128, nb)
    fine = pltpu.VMEM((8, 4, 32, 128), f32)
    fine2 = pltpu.VMEM((2, 8, 4, 32, 128), f32)
    face = pltpu.VMEM((8, 2, 32, 128), f32)
    turned = pltpu.VMEM((8, 4, 16, 128), f32)
    coarse = pltpu.VMEM((8, 32, 128), f32)
    coarse2 = pltpu.VMEM((2, 8, 32, 128), f32)
    owned = pltpu.VMEM((4, 4, 32, 128), f32)
    vmem = pl.BlockSpec(memory_space=pltpu.VMEM)
    scratch = [pltpu.VMEM(state.shape, f32)] * 4 + [pltpu.VMEM(coarse_inverse.shape, f32)]
    scratch += [pltpu.VMEM((2, 8, 32, 128), f32)] + [turned] * 4 + [fine] * 4 + [face] * 4 + [fine] * 3
    scratch += [fine2] * 3 + [fine] * 3
    scratch += [coarse] * 6 + [coarse2, coarse, coarse2] + [coarse] * 3
    scratch += [pltpu.VMEM((2, n, 1, width), f32), pltpu.VMEM((3, 32, 128), f32), fine, owned, owned, turned, turned]
    scratch += [pltpu.SemaphoreType.DMA((72,)), pltpu.SemaphoreType.DMA((72,)), pltpu.SemaphoreType.DMA((5,))]
    shape = jax.ShapeDtypeStruct(state.shape, f32)
    return pl.pallas_call(
        functools.partial(kernel, n, nb),
        out_shape=(shape, shape),
        in_specs=[pl.BlockSpec(memory_space=pltpu.HBM)] * 5,
        out_specs=(vmem, vmem),
        scratch_shapes=scratch,
        compiler_params=pltpu.CompilerParams(collective_id=0, has_side_effects=True, vmem_limit_bytes=60 * 1024 * 1024),
    )(state, permeability, direction, obs_weight, coarse_inverse)


def solution(mesh):
    field = P(("parts", "wide"), "narrow", None)
    return jax.shard_map(
        functools.partial(shards, mesh.shape["wide"] * mesh.shape["narrow"]),
        mesh=mesh,
        in_specs=(field, field, field, field, P("parts", None)),
        out_specs=(field, field),
        check_vma=False,
    )
```

```python
import functools

import jax
import jax.numpy as jnp
from jax import lax
from jax.experimental import pallas as pl
from jax.experimental.pallas import tpu as pltpu
from jax.sharding import PartitionSpec as P

MESH = pl.DeviceIdType.MESH
f32 = jnp.float32
bf16 = jnp.bfloat16

cheb_mid = 1.125
cheb_half = 0.875
first_rho = cheb_half / cheb_mid
second_rho = 1.0 / (2.0 * cheb_mid / cheb_half - first_rho)
step_gain = 2.0 * second_rho / cheb_half
carry_gain = second_rho * first_rho
inv_mid = 1.0 / cheb_mid


def split3(a):
    hi = a.astype(bf16)
    rest = a - hi.astype(f32)
    mid = rest.astype(bf16)
    low = (rest - mid.astype(f32)).astype(bf16)
    return hi, mid, low


def permuted(a, perm):
    parts = [jnp.dot(s, perm, preferred_element_type=f32) for s in split3(a)]
    return parts[0] + (parts[1] + parts[2])


def kernel(n, nb, state_hbm, k_hbm, dir_hbm, w_hbm, inv_hbm, hess_out, inc_out, state_in, k_in, dir_in, w_in, inv_in, stage, t_s, t_k, t_c, t_w, s_r, k_r, c_r, w_r,
           czi, czo, cyi, cyo, cx, dia, inv, b_r, x1_r, x2_r, xa, xb, upd, kc, ccx, ccy, ccz, diac, invc, g_r, y1, y2_r,
           ya, yb, updc, tot, corr, adj, o_inc, o_hess, r_inc, r_hess, send_sem, recv_sem, load_sem):
    wide = lax.axis_index("wide")
    core = lax.axis_index("narrow")
    n_wide = n // 2
    p = 2 * wide + core
    other = 1 - core
    rows = 32
    half = 16
    depth = 128

    def dev(q):
        q = jnp.clip(q, 0, n - 1)
        return {"wide": q // 2, "narrow": q % 2}

    sources = (k_hbm, dir_hbm, state_hbm, w_hbm, inv_hbm)
    loads = [pltpu.make_async_copy(src, dst, load_sem.at[i])
             for i, (src, dst) in enumerate(zip(sources, (k_in, dir_in, state_in, w_in, inv_in)))]
    for load in loads:
        load.start()

    barrier = pltpu.get_barrier_semaphore()

    def greet(d, _):
        q = lax.rem(p + d, n)
        pl.semaphore_signal(barrier, inc=1, device_id={"wide": q // 2, "narrow": q % 2}, device_id_type=MESH)
        return 0

    lax.fori_loop(1, n, greet, 0)

    counter = [0]

    def remote(src, dst, target):
        i = counter[0]
        counter[0] += 1
        return pltpu.make_async_remote_copy(src_ref=src, dst_ref=dst, send_sem=send_sem.at[i], recv_sem=recv_sem.at[i],
                                            device_id=target, device_id_type=MESH)

    has = {-1: p >= 1, 1: p <= n - 2, -2: p >= 2, 2: p <= n - 3}
    chip = {-1: wide >= 1, 1: wide <= n_wide - 2}

    class Halo:
        def __init__(self, moves):
            self.moves = [(off, remote(src, dst, dev(p + off))) for off, src, dst in moves]

        def start(self):
            for off, copy in self.moves:
                pl.when(has[off])(copy.start)

        def recv(self):
            for off, copy in self.moves:
                pl.when(has[-off])(copy.wait_recv)

        def sent(self):
            for off, copy in self.moves:
                pl.when(has[off])(copy.wait_send)

    zf = jnp.zeros((4, rows, depth), f32)
    zc = jnp.zeros((rows, depth), f32)

    @pl.when(p == 0)
    def _():
        for l in (0, 1):
            k_r[l] = zf
            s_r[l] = zf
            c_r[l] = zf
            for cyc in (0, 1):
                b_r[cyc, l] = zf
                x1_r[cyc, l] = zf
                x2_r[cyc, l] = zf
            adj[l] = zf
        for l in (0, 1, 2):
            kc[l] = zc
            for cyc in (0, 1):
                g_r[cyc, l] = zc
                y2_r[cyc, l] = zc

    @pl.when(p == n - 1)
    def _():
        for l in (6, 7):
            k_r[l] = zf
            s_r[l] = zf
            c_r[l] = zf
            for cyc in (0, 1):
                b_r[cyc, l] = zf
                x1_r[cyc, l] = zf
                x2_r[cyc, l] = zf
            adj[l] = zf
        for l in (5, 6, 7):
            kc[l] = zc
            for cyc in (0, 1):
                g_r[cyc, l] = zc
                y2_r[cyc, l] = zc

    @pl.when(p == 1)
    def _():
        kc[0] = zc
        for cyc in (0, 1):
            y2_r[cyc, 0] = zc

    @pl.when(p == n - 2)
    def _():
        kc[7] = zc
        for cyc in (0, 1):
            y2_r[cyc, 7] = zc

    row_i = lax.broadcasted_iota(jnp.int32, (256, 256), 0)
    col_i = lax.broadcasted_iota(jnp.int32, (256, 256), 1)
    apart = jnp.where(row_i == jnp.where(col_i < 128, 2 * col_i, 2 * col_i - 255), 1.0, 0.0).astype(bf16)
    together = jnp.where(col_i == jnp.where(row_i < 128, 2 * row_i, 2 * row_i - 255), 1.0, 0.0).astype(bf16)

    mine = pl.multiple_of(half * core, half)
    theirs = pl.multiple_of(half * other, half)

    def planes(values, t_ref, region):
        flat = permuted(values.reshape(256, 256), apart)
        stage[0] = flat[:, :128].reshape(8, 32, 128)
        stage[1] = flat[:, 128:].reshape(8, 32, 128)
        for yp in range(2):
            for zp in range(2):
                t_ref[:, 2 * yp + zp] = stage[zp, :, pl.ds(yp, half, stride=2), :]
        region[pl.ds(2 - 2 * core, 6), :, pl.ds(mine, half), :] = t_ref[pl.ds(2 * core, 6)]

    loads[0].wait()
    planes(k_in[...], t_k, k_r)
    loads[1].wait()
    planes(k_in[...] * dir_in[...], t_c, c_r)
    loads[2].wait()
    planes(state_in[...], t_s, s_r)

    def first(t_ref, region, deep, extra, skip=0):
        i = counter[0]
        counter[0] += 6
        partner = pltpu.make_async_remote_copy(
            src_ref=t_ref.at[pl.ds((4 - extra) * other, 4 + extra)],
            dst_ref=region.at[pl.ds(2 - extra * other, 4 + extra), :, pl.ds(mine, half), :],
            send_sem=send_sem.at[i], recv_sem=recv_sem.at[i], device_id={"narrow": other}, device_id_type=MESH)
        left = right = None
        if deep:
            left = pltpu.make_async_remote_copy(
                src_ref=t_ref.at[pl.ds(skip, deep)], dst_ref=region.at[pl.ds(6 + skip, deep), :, pl.ds(mine, half), :],
                send_sem=send_sem.at[i + 1], recv_sem=recv_sem.at[i + 2 + core],
                device_id={"wide": jnp.maximum(wide - 1, 0), "narrow": 1}, device_id_type=MESH)
            right = pltpu.make_async_remote_copy(
                src_ref=t_ref.at[pl.ds(8 - skip - deep, deep)], dst_ref=region.at[pl.ds(2 - skip - deep, deep), :, pl.ds(mine, half), :],
                send_sem=send_sem.at[i + 2], recv_sem=recv_sem.at[i + 2 + core],
                device_id={"wide": jnp.minimum(wide + 1, n_wide - 1), "narrow": 0}, device_id_type=MESH)

        def start():
            if deep:
                pl.when(chip[-1])(left.start)
                pl.when(chip[1])(right.start)
            if not skip:
                partner.start()

        def recv():
            if not skip:
                partner.wait_recv()
            if deep:
                arrives = ((core == 0) & chip[-1]) | ((core == 1) & chip[1])

                @pl.when(arrives)
                def _():
                    for c in (0, 1):
                        at = jnp.where(core == 0, 2 - skip - deep, 6 + skip)
                        pltpu.make_async_copy(t_ref.at[pl.ds(0, deep)],
                                              region.at[pl.ds(at, deep), :, pl.ds(half * c, half), :],
                                              recv_sem.at[i + 2 + c]).wait()

        def sent():
            if not skip:
                partner.wait_send()
            if deep:
                pl.when(chip[-1])(left.wait_send)
                pl.when(chip[1])(right.wait_send)

        return start, recv, sent

    firsts = [first(t_k, k_r, 1, 2), first(t_c, c_r, 1, 1), first(t_s, s_r, 1, 1)]
    weight_move = first(t_w, w_r, 0, 0)
    second_k = first(t_k, k_r, 1, 0, 1)

    pl.semaphore_wait(barrier, n - 1)
    for move in firsts:
        move[0]()
    loads[3].wait()
    loads[4].wait()
    planes(w_in[...], t_w, w_r)

    lane_i = lax.broadcasted_iota(jnp.int32, (rows, depth), 1)
    sub_i = lax.broadcasted_iota(jnp.int32, (rows, depth), 0)
    lane_first, lane_last = lane_i == 0, lane_i == depth - 1
    sub_first, sub_last = sub_i == 0, sub_i == rows - 1

    def after(v, axis):
        return pltpu.roll(v, v.shape[axis] - 1, axis)

    def before(v, axis):
        return pltpu.roll(v, 1, axis)

    def after0(v, axis):
        return jnp.where(sub_last if axis == 0 else lane_last, 0.0, after(v, axis))

    def before0(v, axis):
        return jnp.where(sub_first if axis == 0 else lane_first, 0.0, before(v, axis))

    pairs = ((1, ((0, 1), (2, 3))), (0, ((0, 2), (1, 3))))

    def four(ref, *index):
        return [ref[(*index, q)] for q in range(4)]

    def faces(c):
        inner, outer, around = {}, {}, [None] * 4
        for axis, sets in pairs:
            inner[axis], outer[axis] = [], []
            last = sub_last if axis == 0 else lane_last
            for ev, od in sets:
                inner[axis].append(0.5 * (c[ev] + c[od]))
                outer[axis].append(jnp.where(last, 0.0, 0.5 * (c[od] + after(c[ev], axis))))
                se = c[od] + before0(c[od], axis)
                so = c[ev] + after0(c[ev], axis)
                around[ev] = se if around[ev] is None else around[ev] + se
                around[od] = so if around[od] is None else around[od] + so
        return inner, outer, around

    def within(v, inner, outer):
        acc = [None] * 4
        for axis, sets in pairs:
            for i, (ev, od) in enumerate(sets):
                fi, fo = inner[axis][i], outer[axis][i]
                se = fi * v[od] + before(fo * v[od], axis)
                so = fi * v[ev] + fo * after(v[ev], axis)
                acc[ev] = se if acc[ev] is None else acc[ev] + se
                acc[od] = so if acc[od] is None else acc[od] + so
        return acc

    def loop(low, high, body):
        def step(l, _):
            body(l)
            return 0

        lax.fori_loop(low, high, step, 0)

    def cross(l):
        for q in range(4):
            cx[l, q] = 0.5 * (k_r[l, q] + k_r[l + 1, q])

    def prepare(l):
        c = four(k_r, l)
        inner, outer, around = faces(c)
        for i in range(2):
            czi[l, i], czo[l, i] = inner[1][i], outer[1][i]
            cyi[l, i], cyo[l, i] = inner[0][i], outer[0][i]
        layer = 4 * p - 2 + l
        inside = (layer >= 0) & (layer < 4 * n)
        for q in range(4):
            d = 3.0 * c[q] + 0.5 * (around[q] + k_r[l - 1, q] + k_r[l + 1, q])
            dia[l, q] = d
            inv[l, q] = jnp.where(inside, 1.0 / jnp.where(inside, d, 1.0), 0.0)

    def applied(ref, l, *index):
        v = four(ref, *index, l)
        inner = {1: [czi[l, 0], czi[l, 1]], 0: [cyi[l, 0], cyi[l, 1]]}
        outer = {1: [czo[l, 0], czo[l, 1]], 0: [cyo[l, 0], cyo[l, 1]]}
        acc = within(v, inner, outer)
        out = []
        for q in range(4):
            beside = acc[q] + (cx[l, q] * ref[(*index, l + 1, q)] + cx[l - 1, q] * ref[(*index, l - 1, q)])
            out.append(dia[l, q] * v[q] - beside)
        return out

    def source(l):
        c = four(c_r, l)
        inner, outer, around = faces(c)
        v = four(s_r, l)
        acc = within(v, inner, outer)
        for q in range(4):
            up, down = c_r[l + 1, q], c_r[l - 1, q]
            d = 3.0 * c[q] + 0.5 * (around[q] + up + down)
            beside = acc[q] + 0.5 * ((c[q] + up) * s_r[l + 1, q] + (c[q] + down) * s_r[l - 1, q])
            b_r[0, l, q] = beside - d * v[q]

    def start_smooth(l, cyc):
        for q in range(4):
            x1_r[cyc, l, q] = inv[l, q] * b_r[cyc, l, q] * inv_mid

    def end_smooth(l, cyc):
        ax = applied(x1_r, l, cyc)
        for q in range(4):
            x1 = x1_r[cyc, l, q]
            x2_r[cyc, l, q] = x1 + (carry_gain * x1 + step_gain * inv[l, q] * (b_r[cyc, l, q] - ax[q]))

    def whole_sum(v):
        return jnp.sum(jnp.sum(v, axis=0, keepdims=True), axis=1, keepdims=True)

    def coarse_prepare(l):
        c = kc[l]
        up, down = kc[l + 1], kc[l - 1]
        ccy[l] = jnp.where(sub_last, 0.0, 0.125 * (c + after(c, 0)))
        ccz[l] = jnp.where(lane_last, 0.0, 0.125 * (c + after(c, 1)))
        around = after0(c, 0) + before0(c, 0) + after0(c, 1) + before0(c, 1) + up + down
        d = 0.25 * (3.0 * c + 0.5 * around)
        layer = 2 * p - 3 + l
        inside = (layer >= 0) & (layer < 2 * n)
        diac[l] = d
        invc[l] = jnp.where(inside, 1.0 / jnp.where(inside, d, 1.0), 0.0)

    def coarse_cross(l):
        ccx[l] = 0.125 * (kc[l] + kc[l + 1])

    def coarse_applied(get, l):
        v = get(l)
        fy, fz = ccy[l], ccz[l]
        beside = fy * after(v, 0) + before(fy * v, 0) + fz * after(v, 1) + before(fz * v, 1)
        beside = beside + (ccx[l] * get(l + 1) + ccx[l - 1] * get(l - 1))
        return diac[l] * v - beside

    def home(o_ref, t_ref):
        return remote(o_ref.at[:, :, pl.ds(theirs, half), :], t_ref.at[pl.ds(4 * core, 4)], {"narrow": other})

    def assemble(o_ref, t_ref, out_ref):
        t_ref[pl.ds(4 * core, 4)] = o_ref[:, :, pl.ds(mine, half), :]
        for yp in range(2):
            for zp in range(2):
                stage[zp, :, pl.ds(yp, half, stride=2), :] = t_ref[:, 2 * yp + zp]
        flat = jnp.concatenate([stage[0].reshape(256, 128), stage[1].reshape(256, 128)], axis=1)
        out_ref[...] = permuted(flat, together).reshape(8, 32, 256)

    for move in firsts:
        move[1]()

    for j in (0, 1):
        total = None
        for l in (2 + 2 * j, 3 + 2 * j):
            for q in range(4):
                total = k_r[l, q] if total is None else total + k_r[l, q]
        kc[3 + j] = 0.125 * total
    halo_kc = Halo([(-1, kc.at[pl.ds(3, 2)], kc.at[pl.ds(5, 2)]), (1, kc.at[pl.ds(3, 2)], kc.at[pl.ds(1, 2)]),
                    (-2, kc.at[3], kc.at[7]), (2, kc.at[4], kc.at[0])])
    second_k[0]()
    halo_kc.start()
    pending = [halo_kc]

    loop(2, 6, prepare)
    loop(2, 6, source)
    half_row = sub_i < half

    for cyc in (0, 1):
        if cyc == 1:
            def adjoint_source(l):
                for q in range(4):
                    b_r[1, l, q] = -(w_r[l, q] * o_inc[l - 2, q])

            weight_move[1]()
            loop(2, 6, adjoint_source)
        loop(2, 6, functools.partial(start_smooth, cyc=cyc))
        halo_b = Halo([(-1, b_r.at[cyc, 2], b_r.at[cyc, 6]), (1, b_r.at[cyc, 5], b_r.at[cyc, 1])])
        halo_x1 = Halo([(-1, x1_r.at[cyc, 3], x1_r.at[cyc, 7]), (1, x1_r.at[cyc, 4], x1_r.at[cyc, 0])])
        halo_b.start()
        halo_x1.start()
        pending += [halo_b, halo_x1]
        if cyc == 0:
            loop(1, 6, cross)
        else:
            inc_move = home(o_inc, r_inc)
            inc_move.start()
        loop(3, 5, functools.partial(end_smooth, cyc=cyc))
        if cyc == 0:
            second_k[1]()
            cross(0)
            cross(6)
            prepare(1)
            prepare(6)
        halo_b.recv()
        start_smooth(1, cyc)
        start_smooth(6, cyc)
        halo_x2 = Halo([(-1, x2_r.at[cyc, 3], x2_r.at[cyc, 7]), (1, x2_r.at[cyc, 4], x2_r.at[cyc, 0])])
        end_smooth(2, cyc)
        end_smooth(5, cyc)
        halo_x1.recv()
        halo_x2.start()
        end_smooth(1, cyc)
        end_smooth(6, cyc)

        def restrict(j):
            total = None
            for i in (0, 1):
                l = 2 * j - 4 + i
                ax = applied(x2_r, l, cyc)
                for q in range(4):
                    r = b_r[cyc, l, q] - ax[q]
                    total = r if total is None else total + r
            g_r[cyc, j] = 0.125 * total

        loop(3, 5, restrict)
        halo_g = Halo([(-1, g_r.at[cyc, pl.ds(3, 2)], g_r.at[cyc, pl.ds(5, 2)]),
                       (1, g_r.at[cyc, pl.ds(3, 2)], g_r.at[cyc, pl.ds(1, 2)])])
        halo_g.start()
        pending += [halo_g, halo_x2]
        if cyc == 0:
            weight_move[0]()
            halo_kc.recv()
            loop(0, 7, coarse_cross)
            loop(1, 7, coarse_prepare)
        else:
            inc_move.wait_recv()
            assemble(o_inc, r_inc, inc_out)
        halo_g.recv()

        def coarse_start(l):
            y1[l] = invc[l] * g_r[cyc, l] * inv_mid

        def coarse_end(l):
            ay = coarse_applied(lambda i: y1[i], l)
            v = y1[l]
            y2_r[cyc, l] = v + (carry_gain * v + step_gain * invc[l] * (g_r[cyc, l] - ay))

        loop(1, 7, coarse_start)
        loop(2, 6, coarse_end)
        halo_y = Halo([(-1, y2_r.at[cyc, 4], y2_r.at[cyc, 6]), (1, y2_r.at[cyc, 3], y2_r.at[cyc, 1]),
                       (-2, y2_r.at[cyc, 3], y2_r.at[cyc, 7]), (2, y2_r.at[cyc, 4], y2_r.at[cyc, 0])])
        left_over = None
        for l in (3, 4):
            r = g_r[cyc, l] - coarse_applied(lambda i: y2_r[cyc, i], l)
            left_over = r if left_over is None else left_over + r
        low = whole_sum(left_over[:half])
        high = whole_sum(left_over[half:])
        slots = lax.broadcasted_iota(jnp.int32, (1, tot.shape[-1]), 1)
        tot[cyc, 0] = jnp.where(slots == 2 * wide, low, jnp.where(slots == 2 * wide + 1, high, 0.0))
        sem_at = counter[0]
        counter[0] += 1

        def total_copy(d):
            q = lax.rem(p + d, n)
            return pltpu.make_async_remote_copy(
                src_ref=tot.at[cyc, 0], dst_ref=tot.at[cyc, d], send_sem=send_sem.at[sem_at],
                recv_sem=recv_sem.at[sem_at], device_id={"wide": q // 2, "narrow": q % 2}, device_id_type=MESH)

        loop(1, n, lambda d: total_copy(d).start())
        halo_y.start()
        pending.append(halo_y)
        halo_y.recv()
        everyone = tot.at[cyc, pl.ds(1, n - 1)]
        pltpu.make_async_copy(everyone, everyone, recv_sem.at[sem_at]).wait()
        pltpu.make_async_copy(everyone, everyone, send_sem.at[sem_at]).wait()
        totals = jnp.sum(tot[cyc], axis=0)[:, :nb]
        for i in range(3):
            at = jnp.clip(wide + i - 1, 0, n_wide - 1)
            ends = wide + i - 1
            inside = (ends >= 0) & (ends < n_wide)
            values = []
            for h in range(2):
                row = inv_in[pl.ds(2 * at + h, 1), :]
                values.append(jnp.sum(row * totals, axis=1, keepdims=True))
            corr[i] = jnp.where(inside, jnp.where(half_row, values[0], values[1]), 0.0)

        def coarse_add(l):
            ya[l] = y2_r[cyc, l] + corr[(2 * core + 1 + l) // 4]

        def coarse_third(l):
            e = invc[l] * (g_r[cyc, l] - coarse_applied(lambda i: ya[i], l)) * inv_mid
            updc[l] = e
            yb[l] = ya[l] + e

        def coarse_fourth(l):
            r = g_r[cyc, l] - coarse_applied(lambda i: yb[i], l)
            y1[l] = yb[l] + (carry_gain * updc[l] + step_gain * invc[l] * r)

        loop(0, 8, coarse_add)
        loop(1, 7, coarse_third)
        loop(2, 6, coarse_fourth)
        halo_x2.recv()

        def prolong(j):
            y = y1[j]
            for i in (0, 1):
                l = 2 * j - 4 + i
                for q in range(4):
                    xa[l, q] = x2_r[cyc, l, q] + y

        def third(l):
            ax = applied(xa, l)
            for q in range(4):
                e = inv[l, q] * (b_r[cyc, l, q] - ax[q]) * inv_mid
                upd[l, q] = e
                xb[l, q] = xa[l, q] + e

        def fourth(l):
            ax = applied(xb, l)
            for q in range(4):
                r = b_r[cyc, l, q] - ax[q]
                out = xb[l, q] + (carry_gain * upd[l, q] + step_gain * inv[l, q] * r)
                if cyc == 0:
                    o_inc[l - 2, q] = out
                else:
                    adj[l, q] = out

        loop(2, 6, prolong)
        loop(1, 7, third)
        loop(2, 6, fourth)

    halo_adj = Halo([(-1, adj.at[2], adj.at[6]), (1, adj.at[5], adj.at[1])])
    halo_adj.start()
    pending.append(halo_adj)

    def hessian(l):
        s, a = four(s_r, l), four(adj, l)
        acc = [(s[q] - s_r[l + 1, q]) * (a[q] - adj[l + 1, q]) + (s[q] - s_r[l - 1, q]) * (a[q] - adj[l - 1, q])
               for q in range(4)]
        for axis, sets in pairs:
            first_one = sub_first if axis == 0 else lane_first
            for ev, od in sets:
                i = (s[ev] - s[od]) * (a[ev] - a[od])
                o = (s[od] - after0(s[ev], axis)) * (a[od] - after0(a[ev], axis))
                acc[ev] = acc[ev] + i + jnp.where(first_one, s[ev] * a[ev], before(o, axis))
                acc[od] = acc[od] + i + o
        for q in range(4):
            o_hess[l - 2, q] = 0.5 * k_r[l, q] * acc[q]

    loop(3, 5, hessian)
    halo_adj.recv()
    hessian(2)
    hessian(5)

    hess_move = home(o_hess, r_hess)
    hess_move.start()
    hess_move.wait_recv()
    assemble(o_hess, r_hess, hess_out)
    for halo in pending:
        halo.sent()
    for move in firsts + [weight_move, second_k]:
        move[2]()
    inc_move.wait_send()
    hess_move.wait_send()


def shards(n, state, permeability, direction, obs_weight, coarse_inverse):
    nb = coarse_inverse.shape[0]
    width = max(128, nb)
    fine = pltpu.VMEM((8, 4, 32, 128), f32)
    fine2 = pltpu.VMEM((2, 8, 4, 32, 128), f32)
    face = pltpu.VMEM((8, 2, 32, 128), f32)
    turned = pltpu.VMEM((8, 4, 16, 128), f32)
    coarse = pltpu.VMEM((8, 32, 128), f32)
    coarse2 = pltpu.VMEM((2, 8, 32, 128), f32)
    owned = pltpu.VMEM((4, 4, 32, 128), f32)
    vmem = pl.BlockSpec(memory_space=pltpu.VMEM)
    scratch = [pltpu.VMEM(state.shape, f32)] * 4 + [pltpu.VMEM(coarse_inverse.shape, f32)]
    scratch += [pltpu.VMEM((2, 8, 32, 128), f32)] + [turned] * 4 + [fine] * 4 + [face] * 4 + [fine] * 3
    scratch += [fine2] * 3 + [fine] * 3
    scratch += [coarse] * 6 + [coarse2, coarse, coarse2] + [coarse] * 3
    scratch += [pltpu.VMEM((2, n, 1, width), f32), pltpu.VMEM((3, 32, 128), f32), fine, owned, owned, turned, turned]
    scratch += [pltpu.SemaphoreType.DMA((72,)), pltpu.SemaphoreType.DMA((72,)), pltpu.SemaphoreType.DMA((5,))]
    shape = jax.ShapeDtypeStruct(state.shape, f32)
    return pl.pallas_call(
        functools.partial(kernel, n, nb),
        out_shape=(shape, shape),
        in_specs=[pl.BlockSpec(memory_space=pltpu.HBM)] * 5,
        out_specs=(vmem, vmem),
        scratch_shapes=scratch,
        compiler_params=pltpu.CompilerParams(collective_id=0, has_side_effects=True, vmem_limit_bytes=60 * 1024 * 1024),
    )(state, permeability, direction, obs_weight, coarse_inverse)


def solution(mesh):
    field = P(("parts", "wide"), "narrow", None)
    return jax.shard_map(
        functools.partial(shards, mesh.shape["wide"] * mesh.shape["narrow"]),
        mesh=mesh,
        in_specs=(field, field, field, field, P("parts", None)),
        out_specs=(field, field),
        check_vma=False,
    )
```
